256 devices in a mesh: rep: 8 (over x, z_hi), fsdp: 32 (over z_lo, y, core).
Axes of the slice: x: 4, y: 4, z: 8 (z_hi: 2, z_lo: 4; z = z_hi * 4 + z_lo), core: 2. Of those that a mesh axis runs over, the one named last changes fastest.
Arguments:
- tokens: bfloat16 [4096, 4096], P(('rep', 'fsdp')), may hold values from -6 to 6
- upstream: bfloat16 [4096, 14336], P(('rep', 'fsdp')), may hold values from -6 to 6
- blocks: bfloat16 [224, 16, 128, 128], P('fsdp'), may hold values from -0.125 to 0.125
- keep_mask: int32 [32, 112], replicated, may hold values from 0 to 1, as said below
- panel_owner: int32 [112], replicated, may hold values from 0 to 31, as said below
Outputs:
- activation: bfloat16 [4096, 14336], P(('rep', 'fsdp'))
- input_grad: bfloat16 [4096, 4096], P(('rep', 'fsdp'))
- block_grad: bfloat16 [224, 16, 128, 128], P('fsdp')
The draws below stay inside these ranges and needn't reach their ends.
Inputs may be any that keep to these rules, and one draw needn't show every extreme that they name: `keep_mask`: every column panel keeps exactly 16 of its 32 blocks. `panel_owner`: non-decreasing over the panels; a shard owns at most 7 panels, some shard owns exactly 7, and some shard owns none.
All inputs are finite; a program needn't handle non-finite values.
Results may differ from the reference program's by a relative error of at most 0.005.
Values may be sent and summed in bfloat16 or wider, within the bound.
No kernel may reach another device: no remote copies, remote signals or barrier semaphores. Data moves between devices by JAX's collectives and lax.ppermute only.
A program may use at most 128 MiB of HBM per device.

```python
import math
import jax
import jax.numpy as jnp
from jax import lax

D = 4096
FF = 14336
BS = 128
RB = 32
CB = 112
KEEP = 16
PMAX = 7
TOKENS = 4096
N_FSDP = 32


def draw_keep_mask(key, part):
    key = jax.random.fold_in(key, 11)
    column_keys = jax.random.split(key, CB)

    def column(column_key):
        shuffled = jax.random.permutation(column_key, RB)
        return (shuffled < KEEP).astype(jnp.int32)
    return jnp.transpose(jax.vmap(column)(column_keys))


def draw_panel_owner(key, part):
    key = jax.random.fold_in(key, 23)
    order_key, share_key, forced_key, flip_key, move_key = jax.random.split(key, 5)
    pair_count = N_FSDP // 2
    share_low = jax.random.randint(share_key, (pair_count,), 0, PMAX + 1).astype(jnp.int32)
    forced = jax.random.randint(forced_key, (), 0, pair_count).astype(jnp.int32)
    pair_ids = jnp.arange(pair_count, dtype=jnp.int32)
    share_low = jnp.where(pair_ids == forced, PMAX, share_low).astype(jnp.int32)
    flip_bits = jax.random.randint(flip_key, (pair_count,), 0, 2)
    first_count = jnp.where(flip_bits == 1, share_low, PMAX - share_low).astype(jnp.int32)
    second_count = (PMAX - first_count).astype(jnp.int32)
    paired = jnp.stack([first_count, second_count], axis=1).reshape(-1).astype(jnp.int32)
    order = jax.random.permutation(order_key, N_FSDP).astype(jnp.int32)
    counts = jnp.zeros((N_FSDP,), jnp.int32).at[order].set(paired)
    guard_one = order[2 * forced]
    guard_two = order[2 * forced + 1]

    def move_unit(step, counts_now):
        step_key = jax.random.fold_in(move_key, step)
        picks = jax.random.randint(step_key, (2,), 0, N_FSDP).astype(jnp.int32)
        donor = picks[0]
        taker = picks[1]
        allowed = (donor != taker) & (counts_now[donor] > 0) & (counts_now[taker] < PMAX)
        allowed = allowed & (donor != guard_one) & (donor != guard_two)
        allowed = allowed & (taker != guard_one) & (taker != guard_two)
        delta = allowed.astype(jnp.int32)
        counts_now = counts_now.at[donor].add(-delta)
        return counts_now.at[taker].add(delta)
    counts = lax.fori_loop(0, 4 * N_FSDP, move_unit, counts)
    range_ends = jnp.cumsum(counts).astype(jnp.int32)
    panels = jnp.arange(CB, dtype=jnp.int32)
    return jnp.sum((range_ends[None, :] <= panels[:, None]).astype(jnp.int32), axis=1).astype(jnp.int32)


def block_scale(stream_key, shape, shards, least, largest):
    loudness, own = 1.0, jax.random.fold_in(stream_key, 6)
    for axis_at, parts in shards:
        steps = jnp.exp(jax.random.uniform(jax.random.fold_in(own, axis_at), (parts,), jnp.float32, least / len(shards), largest / len(shards)))
        loudness = loudness * jnp.repeat(steps, shape[axis_at] // parts).reshape([-1 if axis == axis_at else 1 for axis in range(len(shape))])
    return loudness


def scatter_about(stream_key, dims, width, bound, shards=(), held_as=jnp.bfloat16):
    drawn = jax.random.normal(stream_key, dims, jnp.float32) * width
    if len(shards) > 0:
        drawn = block_scale(stream_key, dims, shards, -0.22, 0.18) * drawn
    return jnp.clip(drawn, min=-bound, max=bound).astype(held_as)


def setup_inputs(seed: int = 0) -> dict:
    key_list = jax.random.split(jax.random.key(seed), 6)
    return {
        "tokens": scatter_about(key_list[0], (TOKENS, D), 1.0, 6.0, ((0, 256),)),
        "upstream": scatter_about(key_list[1], (TOKENS, FF), 1.0, 6.0, ((0, 256),)),
        "blocks": scatter_about(key_list[2], (N_FSDP * PMAX, KEEP, BS, BS), (KEEP * BS) ** -0.5, 0.125, ((0, 32),)),
        "keep_mask": draw_keep_mask(jax.random.fold_in(key_list[5], 71), 0),
        "panel_owner": draw_panel_owner(jax.random.fold_in(key_list[5], 71), 0),
    }


def layout_tables(keep_mask, panel_owner):
    shard_ids = jnp.arange(N_FSDP, dtype=jnp.int32)
    member = (panel_owner[:, None] == shard_ids[None, :]).astype(jnp.int32)
    counts = lax.optimization_barrier(jnp.sum(member, axis=0)).astype(jnp.int32)
    first_panel = (jnp.cumsum(counts) - counts).astype(jnp.int32)
    slot_ids = jnp.arange(PMAX, dtype=jnp.int32)
    panel_table = jnp.clip(first_panel[:, None] + slot_ids[None, :], 0, CB - 1).astype(jnp.int32)
    slot_live = slot_ids[None, :] < counts[:, None]
    running = jnp.cumsum(keep_mask, axis=0).astype(jnp.int32)
    pick_ids = jnp.arange(KEEP, dtype=jnp.int32)
    kept_rows = lax.optimization_barrier(jnp.sum((running[:, :, None] <= pick_ids[None, None, :]).astype(jnp.int32), axis=0)).astype(jnp.int32)
    panel_ids = jnp.arange(CB, dtype=jnp.int32)
    panel_slot = (panel_owner * PMAX + panel_ids - first_panel[panel_owner]).astype(jnp.int32)
    return (panel_table, slot_live, running, kept_rows, panel_slot)

def reference(tokens, upstream, blocks, keep_mask, panel_owner):
    panel_table, slot_live, running, kept_rows, panel_slot = layout_tables(keep_mask, panel_owner)
    rank = jnp.clip(running - 1, 0, KEEP - 1).astype(jnp.int32)
    placed = blocks[panel_slot[None, :], rank]
    placed = jnp.where(keep_mask[:, :, None, None] == 1, placed, jnp.zeros((), blocks.dtype))
    weight = jnp.transpose(placed, (0, 2, 1, 3)).reshape(D, FF)
    preact = jnp.dot(tokens, weight, preferred_element_type=jnp.float32)
    activation = jax.nn.silu(preact).astype(jnp.bfloat16)
    sigmoid_z = jax.nn.sigmoid(preact)
    slope = sigmoid_z * (1.0 + preact * (1.0 - sigmoid_z))
    dpre = (upstream.astype(jnp.float32) * slope).astype(jnp.bfloat16)
    dpre3 = dpre.reshape(TOKENS, CB, BS)
    weight3 = weight.reshape(D, CB, BS)

    def owner_term(accum_rows, owner_id):
        columns = panel_table[owner_id]
        is_live = slot_live[owner_id]
        picked = jnp.take(dpre3, columns, axis=1)
        picked = jnp.where(is_live[None, :, None], picked, jnp.zeros((), dpre.dtype))
        weights_k = jnp.take(weight3, columns, axis=1)
        term = lax.dot_general(picked.reshape(TOKENS, PMAX * BS), weights_k.reshape(D, PMAX * BS), (((1,), (1,)), ((), ())), preferred_element_type=jnp.float32)
        return (accum_rows + term, None)
    summed, ignored = lax.scan(owner_term, jnp.zeros((TOKENS, D), jnp.float32), jnp.arange(N_FSDP, dtype=jnp.int32))
    input_grad = summed.astype(jnp.bfloat16)
    full_grad = lax.dot_general(tokens, dpre, (((0,), (0,)), ((), ())), preferred_element_type=jnp.float32)
    full4 = full_grad.reshape(RB, BS, CB, BS)
    flat_panels = panel_table.reshape(-1)
    row_ids = kept_rows[flat_panels]
    gathered = full4[row_ids, :, flat_panels[:, None], :]
    scaled = gathered * (1.0 / math.sqrt(TOKENS))
    live_flat = slot_live.reshape(-1)
    block_grad = jnp.where(live_flat[:, None, None, None], scaled, 0.0).astype(jnp.bfloat16)
    return (activation, input_grad, block_grad)
```

```python
import functools
import math

import jax
import jax.numpy as jnp
from jax import lax
from jax.experimental import pallas as pl
from jax.experimental.pallas import tpu as pltpu
from jax.sharding import PartitionSpec as P

NZ, NY, NC = 4, 4, 2
NX, NH = 4, 2
GROUP = 16


def shift_zl(distance):
    return [
        ((z * NY + y) * NC + c, (((z + distance) % NZ) * NY + y) * NC + c)
        for z in range(NZ)
        for y in range(NY)
        for c in range(NC)
    ]


def shift_y(distance):
    return [
        ((z * NY + y) * NC + c, (z * NY + (y + distance) % NY) * NC + c)
        for z in range(NZ)
        for y in range(NY)
        for c in range(NC)
    ]


def swap_c():
    return [(k, k ^ 1) for k in range(NZ * NY * NC)]


def shift_x(distance):
    return [
        (x * NH + h, ((x + distance) % NX) * NH + h) for x in range(NX) for h in range(NH)
    ]


def swap_h():
    return [(r, r ^ 1) for r in range(NX * NH)]


def build_dense(rows_ref, blocks_ref, dense_ref):
    slots, keep, bs = blocks_ref.shape[0], blocks_ref.shape[1], blocks_ref.shape[2]
    dense_ref[...] = jnp.zeros_like(dense_ref)
    for p in range(slots):
        for j in range(keep):
            at = pl.multiple_of(rows_ref[p * keep + j] * bs, bs)
            dense_ref[pl.ds(at, bs), p * bs : (p + 1) * bs] = blocks_ref[p, j]


def forward_kernel(
    rows_ref,
    rank_ref,
    live_ref,
    source_ref,
    own_ref,
    sib_ref,
    blocks_ref,
    ups_ref,
    act_ref,
    dz_ref,
    *rest,
):
    chunk_refs = rest[:NX]
    dense_ref, grads_ref, sems = rest[NX:]
    slots, keep, bs = blocks_ref.shape[0], blocks_ref.shape[1], blocks_ref.shape[2]
    half = own_ref.shape[0]
    row_blocks = own_ref.shape[1] // bs
    tile = 128
    build_dense(rows_ref, blocks_ref, dense_ref)

    for which, tok_ref in enumerate((own_ref, sib_ref)):

        def step(t, carry, which=which, tok_ref=tok_ref):
            row = pl.multiple_of(t * tile, tile)
            z = jnp.dot(
                tok_ref[pl.ds(row, tile), :], dense_ref[...], preferred_element_type=jnp.float32
            )
            sig = jax.nn.sigmoid(z)
            act = (z * sig).astype(jnp.bfloat16)
            slope = sig * (1.0 + z * (1.0 - sig))
            for g in range(tile // GROUP):
                src = source_ref[which * (half // GROUP) + t * (tile // GROUP) + g]
                lo = g * GROUP
                for p in range(slots):
                    cols = slice(p * bs, (p + 1) * bs)
                    act_ref[src, p] = act[lo : lo + GROUP, cols]
                    up = ups_ref[src, p].astype(jnp.float32) * slope[lo : lo + GROUP, cols]
                    up = jnp.where(live_ref[p] == 1, up, 0.0)
                    dz_ref[pl.ds(which * half + row + lo, GROUP), cols] = up.astype(jnp.bfloat16)
            return carry

        lax.fori_loop(0, half // tile, step, 0)

    chunk = slots * keep // NX

    def grad_step(r, carry):
        at = pl.multiple_of(r * bs, bs)
        left = jnp.concatenate([own_ref[:, pl.ds(at, bs)], sib_ref[:, pl.ds(at, bs)]], axis=0)
        grad = lax.dot_general(
            left, dz_ref[...], (((0,), (0,)), ((), ())), preferred_element_type=jnp.float32
        ).astype(jnp.bfloat16)
        for p in range(slots):
            rank = rank_ref[p * row_blocks + r]

            @pl.when(rank >= 0)
            def _(p=p, rank=rank):
                grads_ref[rank] = grad[:, p * bs : (p + 1) * bs]

        return carry

    lax.fori_loop(0, row_blocks, grad_step, 0)
    copies = [
        pltpu.make_async_copy(
            grads_ref.at[pl.ds(d * chunk, chunk)], chunk_refs[d], sems.at[d]
        )
        for d in range(NX)
    ]
    for copy in copies:
        copy.start()
    for copy in copies:
        copy.wait()


def backward_kernel(rows_ref, blocks_ref, dz_ref, own_ref, sib_ref, dense_ref):
    half = own_ref.shape[0]
    tile = 128
    build_dense(rows_ref, blocks_ref, dense_ref)
    for which, out_ref in enumerate((own_ref, sib_ref)):

        def step(t, carry, which=which, out_ref=out_ref):
            row = pl.multiple_of(t * tile, tile)
            grad = lax.dot_general(
                dz_ref[pl.ds(which * half + row, tile), :],
                dense_ref[...],
                (((1,), (1,)), ((), ())),
                preferred_element_type=jnp.float32,
            )
            out_ref[pl.ds(row, tile), :] = grad.astype(jnp.bfloat16)
            return carry

        lax.fori_loop(0, half // tile, step, 0)


def whole():
    return pl.BlockSpec(memory_space=pltpu.VMEM)


def scalars():
    return pl.BlockSpec(memory_space=pltpu.SMEM)


def per_device(tokens, upstream, blocks, keep_mask, panel_owner):
    shard_count = lax.axis_size("fsdp")
    own_index = lax.axis_index("fsdp")
    x_index = lax.axis_index("rep") // NH
    tok_dev, model_width = tokens.shape
    slot_count, keep_count, block_size = blocks.shape[0], blocks.shape[1], blocks.shape[3]
    row_blocks = keep_mask.shape[0]
    panel_count = panel_owner.shape[0]
    half = tok_dev * NZ * NY
    f32, bf16 = jnp.float32, jnp.bfloat16

    shard_ids = jnp.arange(shard_count, dtype=jnp.int32)
    member = (panel_owner[:, None] == shard_ids[None, :]).astype(jnp.int32)
    counts = jnp.sum(member, axis=0)
    first_panel = jnp.cumsum(counts) - counts
    slot_ids = jnp.arange(slot_count, dtype=jnp.int32)
    panel_table = jnp.clip(first_panel[:, None] + slot_ids[None, :], 0, panel_count - 1)
    is_mine = shard_ids == own_index
    own_first = jnp.sum(jnp.where(is_mine, first_panel, 0))
    own_count = jnp.sum(jnp.where(is_mine, counts, 0))
    own_live = (slot_ids < own_count).astype(jnp.int32)
    own_panels = jnp.clip(own_first + slot_ids, 0, panel_count - 1)
    panel_ids = jnp.arange(panel_count, dtype=jnp.int32)
    panel_pick = (panel_ids[None, :] == own_panels[:, None]).astype(jnp.int32)
    running = jnp.cumsum(keep_mask, axis=0)
    own_running = jnp.sum(panel_pick[:, None, :] * running[None, :, :], axis=2)
    own_keep = jnp.sum(panel_pick[:, None, :] * keep_mask[None, :, :], axis=2)
    pick_ids = jnp.arange(keep_count, dtype=jnp.int32)
    own_rows = jnp.sum(
        (own_running[:, :, None] <= pick_ids[None, None, :]).astype(jnp.int32), axis=1
    )
    chunk = slot_count * keep_count // NX
    flat = slot_ids[:, None] * keep_count + own_running - 1
    place = ((flat // chunk - x_index) % NX) * chunk + flat % chunk
    rank = jnp.where(own_keep == 1, place, -1).astype(jnp.int32)
    my_z, my_y, my_c = own_index // (NY * NC), (own_index // NC) % NY, own_index % NC
    away_c = jnp.arange(2, dtype=jnp.int32)[:, None, None]
    away_y = jnp.arange(NY, dtype=jnp.int32)[None, :, None]
    away_z = jnp.arange(NZ, dtype=jnp.int32)[None, None, :]
    source = (((my_z - away_z) % NZ) * NY + (my_y - away_y) % NY) * NC + (my_c + away_c) % NC
    source = source.reshape(-1).astype(jnp.int32)

    along_z = [tokens] + [lax.ppermute(tokens, "fsdp", shift_zl(d)) for d in range(1, NZ)]
    line = jnp.concatenate(along_z, axis=0)
    along_y = [line] + [lax.ppermute(line, "fsdp", shift_y(d)) for d in range(1, NY)]
    tok_own = jnp.concatenate(along_y, axis=0)
    tok_sib = lax.ppermute(tok_own, "fsdp", swap_c())

    upstream_panels = jnp.transpose(upstream.reshape(tok_dev, panel_count, block_size), (1, 0, 2))
    outgoing = jnp.take(upstream_panels, panel_table.reshape(-1), axis=0)
    outgoing = outgoing.reshape(shard_count, slot_count, tok_dev, block_size)
    incoming = lax.all_to_all(outgoing, "fsdp", split_axis=0, concat_axis=0, tiled=True)

    wide = slot_count * block_size
    flops = 2 * 2 * half * model_width * wide
    outs = pl.pallas_call(
        forward_kernel,
        out_shape=(
            jax.ShapeDtypeStruct(incoming.shape, bf16),
            jax.ShapeDtypeStruct((2 * half, wide), bf16),
        )
        + tuple(
            jax.ShapeDtypeStruct((chunk, block_size, block_size), bf16) for _ in range(NX)
        ),
        in_specs=[scalars()] * 4 + [whole()] * 4,
        out_specs=(whole(), whole()) + (pl.BlockSpec(memory_space=pl.ANY),) * NX,
        scratch_shapes=[
            pltpu.VMEM((model_width, wide), bf16),
            pltpu.VMEM((NX * chunk, block_size, block_size), bf16),
            pltpu.SemaphoreType.DMA((NX,)),
        ],
        compiler_params=pltpu.CompilerParams(vmem_limit_bytes=52 * 2**20),
        cost_estimate=pl.CostEstimate(
            flops=2 * flops, bytes_accessed=20 * 2**20, transcendentals=0
        ),
        name="forward_and_weight_grad",
    )(
        own_rows.reshape(-1).astype(jnp.int32),
        rank.reshape(-1),
        own_live,
        source,
        tok_own,
        tok_sib,
        blocks,
        incoming,
    )
    acts, dz, pieces = outs[0], outs[1], outs[2:]

    got = [lax.ppermute(pieces[d], "rep", shift_x(d)) for d in range(1, NX)]

    returned = lax.all_to_all(acts, "fsdp", split_axis=0, concat_axis=0, tiled=True)
    panel_first = jnp.sum(member * first_panel[None, :], axis=1)
    panel_slot = panel_owner * slot_count + panel_ids - panel_first
    act_panels = jnp.take(
        returned.reshape(shard_count * slot_count, tok_dev, block_size), panel_slot, axis=0
    )
    activation_out = jnp.transpose(act_panels, (1, 0, 2)).reshape(tok_dev, panel_count * block_size)

    grad_own, grad_sib = pl.pallas_call(
        backward_kernel,
        out_shape=(jax.ShapeDtypeStruct((half, model_width), bf16),) * 2,
        in_specs=[scalars()] + [whole()] * 2,
        out_specs=(whole(), whole()),
        scratch_shapes=[pltpu.VMEM((model_width, wide), bf16)],
        compiler_params=pltpu.CompilerParams(vmem_limit_bytes=40 * 2**20),
        cost_estimate=pl.CostEstimate(flops=flops, bytes_accessed=10 * 2**20, transcendentals=0),
        name="input_grad",
    )(own_rows.reshape(-1).astype(jnp.int32), blocks, dz)

    from_sib = lax.ppermute(grad_sib, "fsdp", swap_c())
    pair = (grad_own.astype(f32) + from_sib.astype(f32)).astype(bf16)
    pair = pair.reshape(NY, NZ * tok_dev, model_width)
    parts = [lax.ppermute(pair[d], "fsdp", shift_y(-d)) for d in range(1, NY)]
    total = pair[0].astype(f32)
    for part in parts:
        total = total + part.astype(f32)
    total = total.astype(bf16).reshape(NZ, tok_dev, model_width)
    parts = [lax.ppermute(total[d], "fsdp", shift_zl(-d)) for d in range(1, NZ)]
    input_grad = total[0].astype(f32)
    for part in parts:
        input_grad = input_grad + part.astype(f32)
    input_grad = input_grad.astype(bf16)

    along_x = pieces[0].astype(f32)
    for part in got:
        along_x = along_x + part.astype(f32)
    along_x = along_x.astype(bf16)
    other = lax.ppermute(along_x, "rep", swap_h())
    scale = 1.0 / math.sqrt(2 * half * lax.axis_size("rep"))
    mine = ((along_x.astype(f32) + other.astype(f32)) * scale).astype(bf16)
    block_grad = lax.all_gather(
        mine,
        "rep",
        axis=0,
        tiled=True,
        axis_index_groups=[[x * NH + h for x in range(NX)] for h in range(NH)],
    )
    return (activation_out, input_grad, block_grad.reshape(blocks.shape))


def solution(mesh):
    return jax.shard_map(
        per_device,
        mesh=mesh,
        in_specs=(
            P(("rep", "fsdp"), None),
            P(("rep", "fsdp"), None),
            P("fsdp", None, None, None),
            P(),
            P(),
        ),
        out_specs=(P(("rep", "fsdp"), None), P(("rep", "fsdp"), None), P("fsdp", None, None, None)),
        check_vma=False,
    )
```

```python
import functools
import math

import jax
import jax.numpy as jnp
from jax import lax
from jax.experimental import pallas as pl
from jax.experimental.pallas import tpu as pltpu
from jax.sharding import PartitionSpec as P

NZ, NY, NC = 4, 4, 2
NX, NH = 4, 2
GROUP = 16


def shift_zl(distance):
    return [
        ((z * NY + y) * NC + c, (((z + distance) % NZ) * NY + y) * NC + c)
        for z in range(NZ)
        for y in range(NY)
        for c in range(NC)
    ]


def shift_y(distance):
    return [
        ((z * NY + y) * NC + c, (z * NY + (y + distance) % NY) * NC + c)
        for z in range(NZ)
        for y in range(NY)
        for c in range(NC)
    ]


def swap_c():
    return [(k, k ^ 1) for k in range(NZ * NY * NC)]


def shift_x(distance):
    return [
        (x * NH + h, ((x + distance) % NX) * NH + h) for x in range(NX) for h in range(NH)
    ]


def swap_h():
    return [(r, r ^ 1) for r in range(NX * NH)]


def build_dense(rows_ref, first, blocks_ref, dense_ref):
    slots, keep, bs = blocks_ref.shape[0], blocks_ref.shape[1], blocks_ref.shape[2]
    for p in range(slots):
        for j in range(keep):
            at = pl.multiple_of(rows_ref[(first + p) * keep + j] * bs, bs)
            dense_ref[pl.ds(at, bs), p * bs : (p + 1) * bs] = blocks_ref[p, j]


def forward_kernel(first, slots, pieces, rows_ref, place_ref, live_ref, source_ref, *rest):
    token_hbm = rest[:pieces]
    blocks_hbm, ups_hbm = rest[pieces : pieces + 2]
    outs = rest[pieces + 2 :]
    earlier_ref = None
    if first > 0:
        earlier_ref, outs = outs[0], outs[1:]
    act_ref, dz_ref = outs[:2]
    chunk_refs, outs = outs[2 : 2 + NX], outs[2 + NX :]
    if first > 0:
        back_refs, outs = outs[:2], outs[2:]
    tok_ref, blocks_ref, ups_ref, dense_ref, dzt_ref, dzs_ref, grads_ref, in_sems, out_sems = outs
    keep, bs = blocks_ref.shape[1], blocks_ref.shape[2]
    base = blocks_ref.shape[0] - slots
    rows, width = tok_ref.shape
    row_blocks = width // bs
    part = rows // pieces
    tile, span = 512, 1024

    get_blocks = pltpu.make_async_copy(
        blocks_hbm.at[pl.ds(first - base, base + slots)], blocks_ref, in_sems.at[0]
    )
    get_ups = pltpu.make_async_copy(ups_hbm.at[:, pl.ds(first, slots)], ups_ref, in_sems.at[1])
    get_tokens = [
        pltpu.make_async_copy(
            token_hbm[i], tok_ref.at[pl.ds(i * part, part)], in_sems.at[2 + i]
        )
        for i in range(pieces)
    ]
    get_blocks.start()
    for copy in get_tokens:
        copy.start()
    get_ups.start()
    dense_ref[...] = jnp.zeros_like(dense_ref)
    get_blocks.wait()
    build_dense(rows_ref, first - base, blocks_ref, dense_ref)
    get_ups.wait()
    for copy in get_tokens:
        copy.wait()

    def step(t, carry):
        row = pl.multiple_of(t * tile, tile)
        z = jnp.dot(
            tok_ref[pl.ds(row, tile), :],
            dense_ref[:, base * bs :],
            preferred_element_type=jnp.float32,
        )
        sig = jax.nn.sigmoid(z)
        act = (z * sig).astype(jnp.bfloat16)
        slope = sig * (1.0 + z * (1.0 - sig))
        for g in range(tile // GROUP):
            src = source_ref[t * (tile // GROUP) + g]
            lo = g * GROUP
            for p in range(slots):
                cols = slice(p * bs, (p + 1) * bs)
                act_ref[src, p] = act[lo : lo + GROUP, cols]
                up = ups_ref[src, p].astype(jnp.float32) * slope[lo : lo + GROUP, cols]
                up = jnp.where(live_ref[first + p] == 1, up, 0.0)
                dz_ref[pl.ds(row + lo, GROUP), cols] = up.astype(jnp.bfloat16)
        return carry

    lax.fori_loop(0, rows // tile, step, 0)

    dzt_ref[...] = dz_ref[...].T

    def grad_step(r, carry):
        at = pl.multiple_of(r * span, span)
        grad = jnp.dot(
            dzt_ref[...], tok_ref[:, pl.ds(at, span)], preferred_element_type=jnp.float32
        ).astype(jnp.bfloat16)
        for k in range(span // bs):
            for p in range(slots):
                place = place_ref[(first + p) * row_blocks + r * (span // bs) + k]
                grads_ref[place] = grad[p * bs : (p + 1) * bs, k * bs : (k + 1) * bs]
        return carry

    lax.fori_loop(0, width // span, grad_step, 0)
    chunk = slots * keep // NX
    copies = [
        pltpu.make_async_copy(
            grads_ref.at[pl.ds(d * chunk, chunk)], chunk_refs[d], out_sems.at[d]
        )
        for d in range(NX)
    ]
    for copy in copies:
        copy.start()
    if first > 0:
        dzs_ref[:, : base * bs] = earlier_ref[...]
        dzs_ref[:, base * bs :] = dz_ref[...]
        half, wide = rows // 2, 512

        def back_step(t, carry):
            at = pl.multiple_of(t * wide, wide)
            back = lax.dot_general(
                dzs_ref[...],
                dense_ref[pl.ds(at, wide), :],
                (((1,), (1,)), ((), ())),
                preferred_element_type=jnp.float32,
            ).astype(jnp.bfloat16)
            back_refs[0][:, pl.ds(at, wide)] = back[:half]
            back_refs[1][:, pl.ds(at, wide)] = back[half:]
            return carry

        lax.fori_loop(0, width // wide, back_step, 0)
    for copy in copies:
        copy.wait()


def add_kernel(*refs):
    out_ref = refs[-1]
    for i in range(out_ref.shape[0]):
        total = refs[0][i].astype(jnp.float32)
        for ref in refs[1:-1]:
            total = total + ref[i].astype(jnp.float32)
        out_ref[i] = total.T.astype(out_ref.dtype)


def place_kernel(count, *refs):
    start_ref = refs[0]
    part_refs, out_ref, sems = refs[1 : 1 + count], refs[-2], refs[-1]
    copies = [
        pltpu.make_async_copy(
            part, out_ref.at[pl.ds(start_ref[i], part.shape[0])], sems.at[i]
        )
        for i, part in enumerate(part_refs)
    ]
    for copy in copies:
        copy.start()
    for copy in copies:
        copy.wait()


SMALL = pl.CostEstimate(flops=1000, bytes_accessed=1000, transcendentals=0)


def anywhere():
    return pl.BlockSpec(memory_space=pl.ANY)


def add_transposed(arrays):
    return pl.pallas_call(
        add_kernel,
        out_shape=jax.ShapeDtypeStruct(arrays[0].shape, jnp.bfloat16),
        in_specs=[whole()] * len(arrays),
        out_specs=whole(),
        cost_estimate=SMALL,
        compiler_params=pltpu.CompilerParams(vmem_limit_bytes=16 * 2**20),
        name="add_along_x",
    )(*arrays)


def place(starts, total, parts, into=None):
    args = (starts, *parts) + (() if into is None else (into,))
    return pl.pallas_call(
        functools.partial(place_kernel, len(parts)),
        out_shape=jax.ShapeDtypeStruct((total,) + parts[0].shape[1:], parts[0].dtype),
        in_specs=[scalars()] + [anywhere()] * (len(args) - 1),
        out_specs=anywhere(),
        input_output_aliases={} if into is None else {len(args) - 1: 0},
        scratch_shapes=[pltpu.SemaphoreType.DMA((len(parts),))],
        cost_estimate=SMALL,
        compiler_params=pltpu.CompilerParams(vmem_limit_bytes=16 * 2**20),
        name="place_blocks",
    )(*args)


def whole():
    return pl.BlockSpec(memory_space=pltpu.VMEM)


def scalars():
    return pl.BlockSpec(memory_space=pltpu.SMEM)


def per_device(tokens, upstream, blocks, keep_mask, panel_owner):
    shard_count = lax.axis_size("fsdp")
    own_index = lax.axis_index("fsdp")
    x_index = lax.axis_index("rep") // NH
    tok_dev, model_width = tokens.shape
    slot_count, keep_count, block_size = blocks.shape[0], blocks.shape[1], blocks.shape[3]
    row_blocks = keep_mask.shape[0]
    panel_count = panel_owner.shape[0]
    half = tok_dev * NZ * NY
    f32, bf16 = jnp.float32, jnp.bfloat16

    shard_ids = jnp.arange(shard_count, dtype=jnp.int32)
    member = (panel_owner[:, None] == shard_ids[None, :]).astype(jnp.int32)
    counts = jnp.sum(member, axis=0)
    first_panel = jnp.cumsum(counts) - counts
    slot_ids = jnp.arange(slot_count, dtype=jnp.int32)
    panel_table = jnp.clip(first_panel[:, None] + slot_ids[None, :], 0, panel_count - 1)
    is_mine = shard_ids == own_index
    own_first = jnp.sum(jnp.where(is_mine, first_panel, 0))
    own_count = jnp.sum(jnp.where(is_mine, counts, 0))
    own_live = (slot_ids < own_count).astype(jnp.int32)
    own_panels = jnp.clip(own_first + slot_ids, 0, panel_count - 1)
    panel_ids = jnp.arange(panel_count, dtype=jnp.int32)
    panel_pick = (panel_ids[None, :] == own_panels[:, None]).astype(jnp.int32)
    running = jnp.cumsum(keep_mask, axis=0)
    own_running = jnp.sum(panel_pick[:, None, :] * running[None, :, :], axis=2)
    own_keep = jnp.sum(panel_pick[:, None, :] * keep_mask[None, :, :], axis=2)
    pick_ids = jnp.arange(keep_count, dtype=jnp.int32)
    own_rows = jnp.sum(
        (own_running[:, :, None] <= pick_ids[None, None, :]).astype(jnp.int32), axis=1
    )
    sets = ((0, slot_count // 2), (slot_count // 2, slot_count))
    places = []
    for lo, hi in sets:
        chunk = (hi - lo) * keep_count // NX
        flat = (slot_ids[lo:hi, None] - lo) * keep_count + own_running[lo:hi] - 1
        spot = ((flat // chunk - x_index) % NX) * chunk + flat % chunk
        places.append(jnp.where(own_keep[lo:hi] == 1, spot, (hi - lo) * keep_count))
    places = jnp.concatenate(places, axis=0).reshape(-1).astype(jnp.int32)
    rows_flat = own_rows.reshape(-1).astype(jnp.int32)
    my_z, my_y, my_c = own_index // (NY * NC), (own_index // NC) % NY, own_index % NC
    away_c = jnp.arange(2, dtype=jnp.int32)[:, None, None]
    away_y = jnp.arange(NY, dtype=jnp.int32)[None, :, None]
    away_z = jnp.arange(NZ, dtype=jnp.int32)[None, None, :]
    source = (((my_z - away_z) % NZ) * NY + (my_y - away_y) % NY) * NC + (my_c + away_c) % NC
    source = source.reshape(-1).astype(jnp.int32)

    upstream_panels = jnp.transpose(upstream.reshape(tok_dev, panel_count, block_size), (1, 0, 2))
    outgoing = jnp.take(upstream_panels, panel_table.reshape(-1), axis=0)
    outgoing = outgoing.reshape(shard_count, slot_count, tok_dev, block_size)
    outgoing, tokens = lax.optimization_barrier((outgoing, tokens))
    incoming = lax.all_to_all(outgoing, "fsdp", split_axis=0, concat_axis=0, tiled=True)

    along_z = [tokens] + [lax.ppermute(tokens, "fsdp", shift_zl(d)) for d in range(1, NZ)]
    line = jnp.concatenate(along_z, axis=0)
    along_y = [line] + [lax.ppermute(line, "fsdp", shift_y(d)) for d in range(1, NY)]
    along_y[1], incoming = lax.optimization_barrier((along_y[1], incoming))
    runs = along_y + [lax.ppermute(run, "fsdp", swap_c()) for run in along_y]

    acts, dzs, pieces = [], [], []
    for lo, hi in sets:
        slots = hi - lo
        wide = slots * block_size
        chunk = slots * keep_count // NX
        held = slots + len(dzs) * lo
        outs = pl.pallas_call(
            functools.partial(forward_kernel, lo, slots, len(runs)),
            out_shape=(
                jax.ShapeDtypeStruct((shard_count, slots, tok_dev, block_size), bf16),
                jax.ShapeDtypeStruct((2 * half, wide), bf16),
            )
            + tuple(
                jax.ShapeDtypeStruct((chunk, block_size, block_size), bf16) for _ in range(NX)
            )
            + (jax.ShapeDtypeStruct((half, model_width), bf16),) * 2 * len(dzs),
            in_specs=[scalars()] * 4 + [anywhere()] * (len(runs) + 2) + [whole()] * len(dzs),
            out_specs=(whole(), whole()) + (anywhere(),) * NX + (whole(),) * 2 * len(dzs),
            scratch_shapes=[
                pltpu.VMEM((2 * half, model_width), bf16),
                pltpu.VMEM((held, keep_count, block_size, block_size), bf16),
                pltpu.VMEM((shard_count, slots, tok_dev, block_size), bf16),
                pltpu.VMEM((model_width, held * block_size), bf16),
                pltpu.VMEM((wide, 2 * half), bf16),
                pltpu.VMEM((2 * half, held * block_size), bf16),
                pltpu.VMEM((NX * chunk + 1, block_size, block_size), bf16),
                pltpu.SemaphoreType.DMA((len(runs) + 2,)),
                pltpu.SemaphoreType.DMA((NX,)),
            ],
            compiler_params=pltpu.CompilerParams(vmem_limit_bytes=40 * 2**20),
            cost_estimate=SMALL,
            name="forward_and_grads" if dzs else "forward_and_block_grad",
        )(rows_flat, places, own_live, source, *runs, blocks, incoming, *dzs)
        acts.append(outs[0])
        dzs.append(outs[1])
        pieces.append(outs[2 : 2 + NX])
    grad_own, grad_sib = outs[2 + NX :]
    got = [[lax.ppermute(piece[d], "rep", shift_x(d)) for d in range(1, NX)] for piece in pieces]

    scale = 1.0 / math.sqrt(2 * half * lax.axis_size("rep"))
    along = [add_transposed([piece[0]] + parts) for piece, parts in zip(pieces, got)]
    grad_sib, along[0] = lax.optimization_barrier((grad_sib, along[0]))
    other = [lax.ppermute(part, "rep", swap_h()) for part in along]
    other[0], along[1] = lax.optimization_barrier((other[0], along[1]))
    mines = [
        ((part.astype(f32) + more.astype(f32)) * scale).astype(bf16)
        for part, more in zip(along, other)
    ]
    gathered = lax.all_gather(
        mines[0],
        "rep",
        axis=0,
        tiled=True,
        axis_index_groups=[[x * NH + h for x in range(NX)] for h in range(NH)],
    )
    rest = [mines[1]] + [lax.ppermute(mines[1], "rep", shift_x(d)) for d in range(1, NX)]
    acts = jnp.concatenate(acts, axis=1)
    acts, along[0] = lax.optimization_barrier((acts, along[0]))
    returned = lax.all_to_all(acts, "fsdp", split_axis=0, concat_axis=0, tiled=True)
    from_sib = lax.ppermute(grad_sib, "fsdp", swap_c())
    pair = (grad_own.astype(f32) + from_sib.astype(f32)).astype(bf16)
    pair = pair.reshape(NY, NZ * tok_dev, model_width)
    parts = [lax.ppermute(pair[d], "fsdp", shift_y(-d)) for d in range(1, NY)]
    total = pair[0].astype(f32)
    for part in parts:
        total = total + part.astype(f32)
    total = total.astype(bf16).reshape(NZ, tok_dev, model_width)
    total, gathered, returned = lax.optimization_barrier((total, gathered, returned))
    parts = [lax.ppermute(total[d], "fsdp", shift_zl(-d)) for d in range(1, NZ)]
    input_grad = total[0].astype(f32)
    for part in parts:
        input_grad = input_grad + part.astype(f32)
    input_grad = input_grad.astype(bf16)

    panel_first = jnp.sum(member * first_panel[None, :], axis=1)
    panel_slot = panel_owner * slot_count + panel_ids - panel_first
    act_panels = jnp.take(
        returned.reshape(shard_count * slot_count, tok_dev, block_size), panel_slot, axis=0
    )
    activation_out = jnp.transpose(act_panels, (1, 0, 2)).reshape(tok_dev, panel_count * block_size)

    blocks_all = slot_count * keep_count
    block_grad = place(jnp.zeros((1,), jnp.int32), blocks_all, [gathered])
    away = jnp.arange(NX, dtype=jnp.int32)
    starts = sets[1][0] * keep_count + ((x_index - away) % NX) * rest[0].shape[0]
    block_grad = place(starts.astype(jnp.int32), blocks_all, rest, block_grad)
    return (activation_out, input_grad, block_grad.reshape(blocks.shape))


def solution(mesh):
    return jax.shard_map(
        per_device,
        mesh=mesh,
        in_specs=(
            P(("rep", "fsdp"), None),
            P(("rep", "fsdp"), None),
            P("fsdp", None, None, None),
            P(),
            P(),
        ),
        out_specs=(P(("rep", "fsdp"), None), P(("rep", "fsdp"), None), P("fsdp", None, None, None)),
        check_vma=False,
    )
```

```python
import functools
import math

import jax
import jax.numpy as jnp
from jax import lax
from jax.experimental import pallas as pl
from jax.experimental.pallas import tpu as pltpu
from jax.sharding import PartitionSpec as P

NZ, NY, NC = 4, 4, 2
NX, NH = 4, 2
GROUP = 16


def shift_zl(distance):
    return [
        ((z * NY + y) * NC + c, (((z + distance) % NZ) * NY + y) * NC + c)
        for z in range(NZ)
        for y in range(NY)
        for c in range(NC)
    ]


def shift_y(distance):
    return [
        ((z * NY + y) * NC + c, (z * NY + (y + distance) % NY) * NC + c)
        for z in range(NZ)
        for y in range(NY)
        for c in range(NC)
    ]


def swap_c():
    return [(k, k ^ 1) for k in range(NZ * NY * NC)]


def shift_x(distance):
    return [
        (x * NH + h, ((x + distance) % NX) * NH + h) for x in range(NX) for h in range(NH)
    ]


def swap_h():
    return [(r, r ^ 1) for r in range(NX * NH)]


def build_dense(rows_ref, first, blocks_ref, dense_ref):
    slots, keep, bs = blocks_ref.shape[0], blocks_ref.shape[1], blocks_ref.shape[2]
    for p in range(slots):
        for j in range(keep):
            at = pl.multiple_of(rows_ref[(first + p) * keep + j] * bs, bs)
            dense_ref[pl.ds(at, bs), p * bs : (p + 1) * bs] = blocks_ref[p, j]


def forward_kernel(first, slots, pieces, rows_ref, place_ref, live_ref, source_ref, *rest):
    token_hbm = rest[:pieces]
    blocks_hbm, ups_hbm = rest[pieces : pieces + 2]
    outs = rest[pieces + 2 :]
    earlier_ref = None
    if first > 0:
        earlier_ref, outs = outs[0], outs[1:]
    act_ref, dz_ref = outs[:2]
    chunk_refs, outs = outs[2 : 2 + NX], outs[2 + NX :]
    if first > 0:
        back_refs, outs = outs[:2], outs[2:]
    tok_ref, blocks_ref, ups_ref, dense_ref, dzt_ref, dzs_ref, grads_ref, in_sems, out_sems = outs
    keep, bs = blocks_ref.shape[1], blocks_ref.shape[2]
    base = blocks_ref.shape[0] - slots
    rows, width = tok_ref.shape
    row_blocks = width // bs
    part = rows // pieces
    tile, span = 512, 1024

    get_blocks = pltpu.make_async_copy(
        blocks_hbm.at[pl.ds(first - base, base + slots)], blocks_ref, in_sems.at[0]
    )
    get_ups = pltpu.make_async_copy(ups_hbm.at[:, pl.ds(first, slots)], ups_ref, in_sems.at[1])
    get_tokens = [
        pltpu.make_async_copy(
            token_hbm[i], tok_ref.at[pl.ds(i * part, part)], in_sems.at[2 + i]
        )
        for i in range(pieces)
    ]
    get_blocks.start()
    for copy in get_tokens:
        copy.start()
    get_ups.start()
    dense_ref[...] = jnp.zeros_like(dense_ref)
    get_blocks.wait()
    build_dense(rows_ref, first - base, blocks_ref, dense_ref)
    get_ups.wait()
    for copy in get_tokens:
        copy.wait()

    def step(t, carry):
        row = pl.multiple_of(t * tile, tile)
        z = jnp.dot(
            tok_ref[pl.ds(row, tile), :],
            dense_ref[:, base * bs :],
            preferred_element_type=jnp.float32,
        )
        sig = jax.nn.sigmoid(z)
        act = (z * sig).astype(jnp.bfloat16)
        slope = sig * (1.0 + z * (1.0 - sig))
        for g in range(tile // GROUP):
            src = source_ref[t * (tile // GROUP) + g]
            lo = g * GROUP
            for p in range(slots):
                cols = slice(p * bs, (p + 1) * bs)
                act_ref[src, p] = act[lo : lo + GROUP, cols]
                up = ups_ref[src, p].astype(jnp.float32) * slope[lo : lo + GROUP, cols]
                up = jnp.where(live_ref[first + p] == 1, up, 0.0)
                dz_ref[pl.ds(row + lo, GROUP), cols] = up.astype(jnp.bfloat16)
        return carry

    lax.fori_loop(0, rows // tile, step, 0)

    dzt_ref[...] = dz_ref[...].T

    def grad_step(r, carry):
        at = pl.multiple_of(r * span, span)
        grad = jnp.dot(
            dzt_ref[...], tok_ref[:, pl.ds(at, span)], preferred_element_type=jnp.float32
        ).astype(jnp.bfloat16)
        for k in range(span // bs):
            for p in range(slots):
                place = place_ref[(first + p) * row_blocks + r * (span // bs) + k]
                grads_ref[place] = grad[p * bs : (p + 1) * bs, k * bs : (k + 1) * bs]
        return carry

    lax.fori_loop(0, width // span, grad_step, 0)
    chunk = slots * keep // NX
    copies = [
        pltpu.make_async_copy(
            grads_ref.at[pl.ds(d * chunk, chunk)], chunk_refs[d], out_sems.at[d]
        )
        for d in range(NX)
    ]
    for copy in copies:
        copy.start()
    if first > 0:
        dzs_ref[:, : base * bs] = earlier_ref[...]
        dzs_ref[:, base * bs :] = dz_ref[...]
        half, wide = rows // 2, 512

        def back_step(t, carry):
            at = pl.multiple_of(t * wide, wide)
            back = lax.dot_general(
                dzs_ref[...],
                dense_ref[pl.ds(at, wide), :],
                (((1,), (1,)), ((), ())),
                preferred_element_type=jnp.float32,
            ).astype(jnp.bfloat16)
            back_refs[0][:, pl.ds(at, wide)] = back[:half]
            back_refs[1][:, pl.ds(at, wide)] = back[half:]
            return carry

        lax.fori_loop(0, width // wide, back_step, 0)
    for copy in copies:
        copy.wait()


def add_kernel(*refs):
    out_ref = refs[-1]
    for i in range(out_ref.shape[0]):
        total = refs[0][i].astype(jnp.float32)
        for ref in refs[1:-1]:
            total = total + ref[i].astype(jnp.float32)
        out_ref[i] = total.T.astype(out_ref.dtype)


def place_kernel(count, *refs):
    start_ref = refs[0]
    part_refs, out_ref, sems = refs[1 : 1 + count], refs[-2], refs[-1]
    copies = [
        pltpu.make_async_copy(
            part, out_ref.at[pl.ds(start_ref[i], part.shape[0])], sems.at[i]
        )
        for i, part in enumerate(part_refs)
    ]
    for copy in copies:
        copy.start()
    for copy in copies:
        copy.wait()


SMALL = pl.CostEstimate(flops=1000, bytes_accessed=1000, transcendentals=0)


def anywhere():
    return pl.BlockSpec(memory_space=pl.ANY)


def add_transposed(arrays):
    return pl.pallas_call(
        add_kernel,
        out_shape=jax.ShapeDtypeStruct(arrays[0].shape, jnp.bfloat16),
        in_specs=[whole()] * len(arrays),
        out_specs=whole(),
        cost_estimate=SMALL,
        compiler_params=pltpu.CompilerParams(vmem_limit_bytes=16 * 2**20),
        name="add_along_x",
    )(*arrays)


def place(starts, total, parts, into=None):
    args = (starts, *parts) + (() if into is None else (into,))
    return pl.pallas_call(
        functools.partial(place_kernel, len(parts)),
        out_shape=jax.ShapeDtypeStruct((total,) + parts[0].shape[1:], parts[0].dtype),
        in_specs=[scalars()] + [whole()] * len(parts) + [anywhere()] * (len(args) - 1 - len(parts)),
        out_specs=anywhere(),
        input_output_aliases={} if into is None else {len(args) - 1: 0},
        scratch_shapes=[pltpu.SemaphoreType.DMA((len(parts),))],
        cost_estimate=SMALL,
        compiler_params=pltpu.CompilerParams(vmem_limit_bytes=16 * 2**20),
        name="place_blocks",
    )(*args)


def whole():
    return pl.BlockSpec(memory_space=pltpu.VMEM)


def scalars():
    return pl.BlockSpec(memory_space=pltpu.SMEM)


def per_device(tokens, upstream, blocks, keep_mask, panel_owner):
    shard_count = lax.axis_size("fsdp")
    own_index = lax.axis_index("fsdp")
    x_index = lax.axis_index("rep") // NH
    tok_dev, model_width = tokens.shape
    slot_count, keep_count, block_size = blocks.shape[0], blocks.shape[1], blocks.shape[3]
    row_blocks = keep_mask.shape[0]
    panel_count = panel_owner.shape[0]
    half = tok_dev * NZ * NY
    f32, bf16 = jnp.float32, jnp.bfloat16

    shard_ids = jnp.arange(shard_count, dtype=jnp.int32)
    member = (panel_owner[:, None] == shard_ids[None, :]).astype(jnp.int32)
    counts = jnp.sum(member, axis=0)
    first_panel = jnp.cumsum(counts) - counts
    slot_ids = jnp.arange(slot_count, dtype=jnp.int32)
    panel_table = jnp.clip(first_panel[:, None] + slot_ids[None, :], 0, panel_count - 1)
    is_mine = shard_ids == own_index
    own_first = jnp.sum(jnp.where(is_mine, first_panel, 0))
    own_count = jnp.sum(jnp.where(is_mine, counts, 0))
    own_live = (slot_ids < own_count).astype(jnp.int32)
    own_panels = jnp.clip(own_first + slot_ids, 0, panel_count - 1)
    panel_ids = jnp.arange(panel_count, dtype=jnp.int32)
    panel_pick = (panel_ids[None, :] == own_panels[:, None]).astype(jnp.int32)
    running = jnp.cumsum(keep_mask, axis=0)
    own_running = jnp.sum(panel_pick[:, None, :] * running[None, :, :], axis=2)
    own_keep = jnp.sum(panel_pick[:, None, :] * keep_mask[None, :, :], axis=2)
    pick_ids = jnp.arange(keep_count, dtype=jnp.int32)
    own_rows = jnp.sum(
        (own_running[:, :, None] <= pick_ids[None, None, :]).astype(jnp.int32), axis=1
    )
    sets = ((0, slot_count // 2), (slot_count // 2, slot_count))
    places = []
    for lo, hi in sets:
        chunk = (hi - lo) * keep_count // NX
        flat = (slot_ids[lo:hi, None] - lo) * keep_count + own_running[lo:hi] - 1
        spot = ((flat // chunk - x_index) % NX) * chunk + flat % chunk
        places.append(jnp.where(own_keep[lo:hi] == 1, spot, (hi - lo) * keep_count))
    places = jnp.concatenate(places, axis=0).reshape(-1).astype(jnp.int32)
    rows_flat = own_rows.reshape(-1).astype(jnp.int32)
    my_z, my_y, my_c = own_index // (NY * NC), (own_index // NC) % NY, own_index % NC
    away_c = jnp.arange(2, dtype=jnp.int32)[:, None, None]
    away_y = jnp.arange(NY, dtype=jnp.int32)[None, :, None]
    away_z = jnp.arange(NZ, dtype=jnp.int32)[None, None, :]
    source = (((my_z - away_z) % NZ) * NY + (my_y - away_y) % NY) * NC + (my_c + away_c) % NC
    source = source.reshape(-1).astype(jnp.int32)

    upstream_panels = jnp.transpose(upstream.reshape(tok_dev, panel_count, block_size), (1, 0, 2))
    outgoing = jnp.take(upstream_panels, panel_table.reshape(-1), axis=0)
    outgoing = outgoing.reshape(shard_count, slot_count, tok_dev, block_size)
    outgoing, tokens = lax.optimization_barrier((outgoing, tokens))
    incoming = lax.all_to_all(outgoing, "fsdp", split_axis=0, concat_axis=0, tiled=True)

    along_z = [tokens] + [lax.ppermute(tokens, "fsdp", shift_zl(d)) for d in range(1, NZ)]
    line = jnp.concatenate(along_z, axis=0)
    along_y = [line] + [lax.ppermute(line, "fsdp", shift_y(d)) for d in range(1, NY)]
    along_y[1], incoming = lax.optimization_barrier((along_y[1], incoming))
    runs = along_y + [lax.ppermute(run, "fsdp", swap_c()) for run in along_y]

    acts, dzs, pieces = [], [], []
    for lo, hi in sets:
        slots = hi - lo
        wide = slots * block_size
        chunk = slots * keep_count // NX
        held = slots + len(dzs) * lo
        outs = pl.pallas_call(
            functools.partial(forward_kernel, lo, slots, len(runs)),
            out_shape=(
                jax.ShapeDtypeStruct((shard_count, slots, tok_dev, block_size), bf16),
                jax.ShapeDtypeStruct((2 * half, wide), bf16),
            )
            + tuple(
                jax.ShapeDtypeStruct((chunk, block_size, block_size), bf16) for _ in range(NX)
            )
            + (jax.ShapeDtypeStruct((half, model_width), bf16),) * 2 * len(dzs),
            in_specs=[scalars()] * 4 + [anywhere()] * (len(runs) + 2) + [whole()] * len(dzs),
            out_specs=(whole(), whole()) + (anywhere(),) * NX + (whole(),) * 2 * len(dzs),
            scratch_shapes=[
                pltpu.VMEM((2 * half, model_width), bf16),
                pltpu.VMEM((held, keep_count, block_size, block_size), bf16),
                pltpu.VMEM((shard_count, slots, tok_dev, block_size), bf16),
                pltpu.VMEM((model_width, held * block_size), bf16),
                pltpu.VMEM((wide, 2 * half), bf16),
                pltpu.VMEM((2 * half, held * block_size), bf16),
                pltpu.VMEM((NX * chunk + 1, block_size, block_size), bf16),
                pltpu.SemaphoreType.DMA((len(runs) + 2,)),
                pltpu.SemaphoreType.DMA((NX,)),
            ],
            compiler_params=pltpu.CompilerParams(vmem_limit_bytes=40 * 2**20),
            cost_estimate=SMALL,
            name="forward_and_grads" if dzs else "forward_and_block_grad",
        )(rows_flat, places, own_live, source, *runs, blocks, incoming, *dzs)
        acts.append(outs[0])
        dzs.append(outs[1])
        pieces.append(outs[2 : 2 + NX])
    grad_own, grad_sib = outs[2 + NX :]
    got = [[lax.ppermute(piece[d], "rep", shift_x(d)) for d in range(1, NX)] for piece in pieces]

    scale = 1.0 / math.sqrt(2 * half * lax.axis_size("rep"))
    along = [add_transposed([piece[0]] + parts) for piece, parts in zip(pieces, got)]
    grad_sib, along[0] = lax.optimization_barrier((grad_sib, along[0]))
    other = [lax.ppermute(part, "rep", swap_h()) for part in along]
    mines = [
        ((part.astype(f32) + more.astype(f32)) * scale).astype(bf16)
        for part, more in zip(along, other)
    ]
    gathered = lax.all_gather(
        mines[0],
        "rep",
        axis=0,
        tiled=True,
        axis_index_groups=[[x * NH + h for x in range(NX)] for h in range(NH)],
    )
    rest = [mines[1]] + [lax.ppermute(mines[1], "rep", shift_x(d)) for d in range(1, NX)]
    acts = jnp.concatenate(acts, axis=1)
    acts, mines[0] = lax.optimization_barrier((acts, mines[0]))
    returned = lax.all_to_all(acts, "fsdp", split_axis=0, concat_axis=0, tiled=True)
    from_sib = lax.ppermute(grad_sib, "fsdp", swap_c())
    pair = (grad_own.astype(f32) + from_sib.astype(f32)).astype(bf16)
    pair = pair.reshape(NY, NZ * tok_dev, model_width)
    parts = [lax.ppermute(pair[d], "fsdp", shift_y(-d)) for d in range(1, NY)]
    total = pair[0].astype(f32)
    for part in parts:
        total = total + part.astype(f32)
    total = total.astype(bf16).reshape(NZ, tok_dev, model_width)
    total, gathered, returned = lax.optimization_barrier((total, gathered, returned))
    parts = [lax.ppermute(total[d], "fsdp", shift_zl(-d)) for d in range(1, NZ)]
    input_grad = total[0].astype(f32)
    for part in parts:
        input_grad = input_grad + part.astype(f32)
    input_grad = input_grad.astype(bf16)

    panel_first = jnp.sum(member * first_panel[None, :], axis=1)
    panel_slot = panel_owner * slot_count + panel_ids - panel_first
    act_panels = jnp.take(
        returned.reshape(shard_count * slot_count, tok_dev, block_size), panel_slot, axis=0
    )
    activation_out = jnp.transpose(act_panels, (1, 0, 2)).reshape(tok_dev, panel_count * block_size)

    blocks_all = slot_count * keep_count
    block_grad = place(jnp.zeros((1,), jnp.int32), blocks_all, [gathered])
    away = jnp.arange(NX, dtype=jnp.int32)
    starts = sets[1][0] * keep_count + ((x_index - away) % NX) * rest[0].shape[0]
    block_grad = place(starts.astype(jnp.int32), blocks_all, rest, block_grad)
    return (activation_out, input_grad, block_grad.reshape(blocks.shape))


def solution(mesh):
    return jax.shard_map(
        per_device,
        mesh=mesh,
        in_specs=(
            P(("rep", "fsdp"), None),
            P(("rep", "fsdp"), None),
            P("fsdp", None, None, None),
            P(),
            P(),
        ),
        out_specs=(P(("rep", "fsdp"), None), P(("rep", "fsdp"), None), P("fsdp", None, None, None)),
        check_vma=False,
    )
```

```python
import functools
import math

import jax
import jax.numpy as jnp
from jax import lax
from jax.experimental import pallas as pl
from jax.experimental.pallas import tpu as pltpu
from jax.sharding import PartitionSpec as P

NZ, NY, NC = 4, 4, 2
NX, NH = 4, 2
GROUP = 16


def shift_zl(distance):
    return [
        ((z * NY + y) * NC + c, (((z + distance) % NZ) * NY + y) * NC + c)
        for z in range(NZ)
        for y in range(NY)
        for c in range(NC)
    ]


def shift_y(distance):
    return [
        ((z * NY + y) * NC + c, (z * NY + (y + distance) % NY) * NC + c)
        for z in range(NZ)
        for y in range(NY)
        for c in range(NC)
    ]


def swap_c():
    return [(k, k ^ 1) for k in range(NZ * NY * NC)]


def shift_x(distance):
    return [
        (x * NH + h, ((x + distance) % NX) * NH + h) for x in range(NX) for h in range(NH)
    ]


def swap_h():
    return [(r, r ^ 1) for r in range(NX * NH)]


def build_dense(rows_ref, first, blocks_ref, dense_ref):
    slots, keep, bs = blocks_ref.shape[0], blocks_ref.shape[1], blocks_ref.shape[2]
    for p in range(slots):
        for j in range(keep):
            at = pl.multiple_of(rows_ref[(first + p) * keep + j] * bs, bs)
            dense_ref[pl.ds(at, bs), p * bs : (p + 1) * bs] = blocks_ref[p, j]


def forward_kernel(first, slots, pieces, rows_ref, place_ref, live_ref, source_ref, *rest):
    token_hbm = rest[:pieces]
    blocks_hbm, ups_hbm = rest[pieces : pieces + 2]
    outs = rest[pieces + 2 :]
    earlier_ref = None
    if first > 0:
        earlier_ref, outs = outs[0], outs[1:]
    act_ref, dz_ref = outs[:2]
    chunk_refs, outs = outs[2 : 2 + NX], outs[2 + NX :]
    if first > 0:
        back_refs, outs = outs[:2], outs[2:]
    tok_ref, blocks_ref, ups_ref, dense_ref, dzt_ref, dzs_ref, grads_ref, in_sems, out_sems = outs
    keep, bs = blocks_ref.shape[1], blocks_ref.shape[2]
    base = blocks_ref.shape[0] - slots
    rows, width = tok_ref.shape
    row_blocks = width // bs
    part = rows // pieces
    tile, span = 512, 1024

    get_blocks = pltpu.make_async_copy(
        blocks_hbm.at[pl.ds(first - base, base + slots)], blocks_ref, in_sems.at[0]
    )
    get_ups = pltpu.make_async_copy(ups_hbm.at[:, pl.ds(first, slots)], ups_ref, in_sems.at[1])
    get_tokens = [
        pltpu.make_async_copy(
            token_hbm[i], tok_ref.at[pl.ds(i * part, part)], in_sems.at[2 + i]
        )
        for i in range(pieces)
    ]
    get_blocks.start()
    for copy in get_tokens:
        copy.start()
    get_ups.start()
    dense_ref[...] = jnp.zeros_like(dense_ref)
    get_blocks.wait()
    build_dense(rows_ref, first - base, blocks_ref, dense_ref)
    get_ups.wait()
    for copy in get_tokens:
        copy.wait()

    def step(t, carry):
        row = pl.multiple_of(t * tile, tile)
        z = jnp.dot(
            tok_ref[pl.ds(row, tile), :],
            dense_ref[:, base * bs :],
            preferred_element_type=jnp.float32,
        )
        sig = jax.nn.sigmoid(z)
        act = (z * sig).astype(jnp.bfloat16)
        slope = sig * (1.0 + z * (1.0 - sig))
        for g in range(tile // GROUP):
            src = source_ref[t * (tile // GROUP) + g]
            lo = g * GROUP
            for p in range(slots):
                cols = slice(p * bs, (p + 1) * bs)
                act_ref[src, p] = act[lo : lo + GROUP, cols]
                up = ups_ref[src, p].astype(jnp.float32) * slope[lo : lo + GROUP, cols]
                up = jnp.where(live_ref[first + p] == 1, up, 0.0)
                dz_ref[pl.ds(row + lo, GROUP), cols] = up.astype(jnp.bfloat16)
        return carry

    lax.fori_loop(0, rows // tile, step, 0)

    dzt_ref[...] = dz_ref[...].T

    def grad_step(r, carry):
        at = pl.multiple_of(r * span, span)
        grad = jnp.dot(
            dzt_ref[...], tok_ref[:, pl.ds(at, span)], preferred_element_type=jnp.float32
        ).astype(jnp.bfloat16)
        for k in range(span // bs):
            for p in range(slots):
                place = place_ref[(first + p) * row_blocks + r * (span // bs) + k]
                grads_ref[place] = grad[p * bs : (p + 1) * bs, k * bs : (k + 1) * bs]
        return carry

    lax.fori_loop(0, width // span, grad_step, 0)
    chunk = slots * keep // NX
    copies = [
        pltpu.make_async_copy(
            grads_ref.at[pl.ds(d * chunk, chunk)], chunk_refs[d], out_sems.at[d]
        )
        for d in range(NX)
    ]
    for copy in copies:
        copy.start()
    if first > 0:
        dzs_ref[:, : base * bs] = earlier_ref[...]
        dzs_ref[:, base * bs :] = dz_ref[...]
        half, wide = rows // 2, 512

        def back_step(t, carry):
            at = pl.multiple_of(t * wide, wide)
            back = lax.dot_general(
                dzs_ref[...],
                dense_ref[pl.ds(at, wide), :],
                (((1,), (1,)), ((), ())),
                preferred_element_type=jnp.float32,
            ).astype(jnp.bfloat16)
            back_refs[0][:, pl.ds(at, wide)] = back[:half]
            back_refs[1][:, pl.ds(at, wide)] = back[half:]
            return carry

        lax.fori_loop(0, width // wide, back_step, 0)
    for copy in copies:
        copy.wait()


def add_kernel(*refs):
    out_ref = refs[-1]
    for i in range(out_ref.shape[0]):
        total = refs[0][i].astype(jnp.float32)
        for ref in refs[1:-1]:
            total = total + ref[i].astype(jnp.float32)
        out_ref[i] = total.T.astype(out_ref.dtype)


def place_kernel(count, *refs):
    start_ref = refs[0]
    part_refs, out_ref, sems = refs[1 : 1 + count], refs[-2], refs[-1]
    copies = [
        pltpu.make_async_copy(
            part, out_ref.at[pl.ds(start_ref[i], part.shape[0])], sems.at[i]
        )
        for i, part in enumerate(part_refs)
    ]
    for copy in copies:
        copy.start()
    for copy in copies:
        copy.wait()


SMALL = pl.CostEstimate(flops=1000, bytes_accessed=1000, transcendentals=0)


def anywhere():
    return pl.BlockSpec(memory_space=pl.ANY)


def add_transposed(arrays):
    return pl.pallas_call(
        add_kernel,
        out_shape=jax.ShapeDtypeStruct(arrays[0].shape, jnp.bfloat16),
        in_specs=[whole()] * len(arrays),
        out_specs=whole(),
        cost_estimate=SMALL,
        compiler_params=pltpu.CompilerParams(vmem_limit_bytes=16 * 2**20),
        name="add_along_x",
    )(*arrays)


def place(starts, total, parts, into=None):
    args = (starts, *parts) + (() if into is None else (into,))
    return pl.pallas_call(
        functools.partial(place_kernel, len(parts)),
        out_shape=jax.ShapeDtypeStruct((total,) + parts[0].shape[1:], parts[0].dtype),
        in_specs=[scalars()] + [whole()] * len(parts) + [anywhere()] * (len(args) - 1 - len(parts)),
        out_specs=anywhere(),
        input_output_aliases={} if into is None else {len(args) - 1: 0},
        scratch_shapes=[pltpu.SemaphoreType.DMA((len(parts),))],
        cost_estimate=SMALL,
        compiler_params=pltpu.CompilerParams(vmem_limit_bytes=16 * 2**20),
        name="place_blocks",
    )(*args)


def whole():
    return pl.BlockSpec(memory_space=pltpu.VMEM)


def scalars():
    return pl.BlockSpec(memory_space=pltpu.SMEM)


def per_device(tokens, upstream, blocks, keep_mask, panel_owner):
    shard_count = lax.axis_size("fsdp")
    own_index = lax.axis_index("fsdp")
    x_index = lax.axis_index("rep") // NH
    tok_dev, model_width = tokens.shape
    slot_count, keep_count, block_size = blocks.shape[0], blocks.shape[1], blocks.shape[3]
    row_blocks = keep_mask.shape[0]
    panel_count = panel_owner.shape[0]
    half = tok_dev * NZ * NY
    f32, bf16 = jnp.float32, jnp.bfloat16

    shard_ids = jnp.arange(shard_count, dtype=jnp.int32)
    member = (panel_owner[:, None] == shard_ids[None, :]).astype(jnp.int32)
    counts = jnp.sum(member, axis=0)
    first_panel = jnp.cumsum(counts) - counts
    slot_ids = jnp.arange(slot_count, dtype=jnp.int32)
    panel_table = jnp.clip(first_panel[:, None] + slot_ids[None, :], 0, panel_count - 1)
    is_mine = shard_ids == own_index
    own_first = jnp.sum(jnp.where(is_mine, first_panel, 0))
    own_count = jnp.sum(jnp.where(is_mine, counts, 0))
    own_live = (slot_ids < own_count).astype(jnp.int32)
    own_panels = jnp.clip(own_first + slot_ids, 0, panel_count - 1)
    panel_ids = jnp.arange(panel_count, dtype=jnp.int32)
    panel_pick = (panel_ids[None, :] == own_panels[:, None]).astype(jnp.int32)
    running = jnp.cumsum(keep_mask, axis=0)
    own_running = jnp.sum(panel_pick[:, None, :] * running[None, :, :], axis=2)
    own_keep = jnp.sum(panel_pick[:, None, :] * keep_mask[None, :, :], axis=2)
    pick_ids = jnp.arange(keep_count, dtype=jnp.int32)
    own_rows = jnp.sum(
        (own_running[:, :, None] <= pick_ids[None, None, :]).astype(jnp.int32), axis=1
    )
    sets = ((0, slot_count // 2), (slot_count // 2, slot_count))
    places = []
    for lo, hi in sets:
        chunk = (hi - lo) * keep_count // NX
        flat = (slot_ids[lo:hi, None] - lo) * keep_count + own_running[lo:hi] - 1
        spot = ((flat // chunk - x_index) % NX) * chunk + flat % chunk
        places.append(jnp.where(own_keep[lo:hi] == 1, spot, (hi - lo) * keep_count))
    places = jnp.concatenate(places, axis=0).reshape(-1).astype(jnp.int32)
    rows_flat = own_rows.reshape(-1).astype(jnp.int32)
    my_z, my_y, my_c = own_index // (NY * NC), (own_index // NC) % NY, own_index % NC
    away_c = jnp.arange(2, dtype=jnp.int32)[:, None, None]
    away_y = jnp.arange(NY, dtype=jnp.int32)[None, :, None]
    away_z = jnp.arange(NZ, dtype=jnp.int32)[None, None, :]
    source = (((my_z - away_z) % NZ) * NY + (my_y - away_y) % NY) * NC + (my_c + away_c) % NC
    source = source.reshape(-1).astype(jnp.int32)

    upstream_panels = jnp.transpose(upstream.reshape(tok_dev, panel_count, block_size), (1, 0, 2))
    outgoing = jnp.take(upstream_panels, panel_table.reshape(-1), axis=0)
    outgoing = outgoing.reshape(shard_count, slot_count, tok_dev, block_size)
    outgoing, tokens = lax.optimization_barrier((outgoing, tokens))
    incoming = lax.all_to_all(outgoing, "fsdp", split_axis=0, concat_axis=0, tiled=True)

    along_z = [tokens] + [lax.ppermute(tokens, "fsdp", shift_zl(d)) for d in range(1, NZ)]
    line = jnp.concatenate(along_z, axis=0)
    along_y = [line] + [lax.ppermute(line, "fsdp", shift_y(d)) for d in range(1, NY)]
    along_y[1], incoming = lax.optimization_barrier((along_y[1], incoming))
    runs = along_y + [lax.ppermute(run, "fsdp", swap_c()) for run in along_y]

    acts, dzs, pieces = [], [], []
    for lo, hi in sets:
        slots = hi - lo
        wide = slots * block_size
        chunk = slots * keep_count // NX
        held = slots + len(dzs) * lo
        outs = pl.pallas_call(
            functools.partial(forward_kernel, lo, slots, len(runs)),
            out_shape=(
                jax.ShapeDtypeStruct((shard_count, slots, tok_dev, block_size), bf16),
                jax.ShapeDtypeStruct((2 * half, wide), bf16),
            )
            + tuple(
                jax.ShapeDtypeStruct((chunk, block_size, block_size), bf16) for _ in range(NX)
            )
            + (jax.ShapeDtypeStruct((half, model_width), bf16),) * 2 * len(dzs),
            in_specs=[scalars()] * 4 + [anywhere()] * (len(runs) + 2) + [whole()] * len(dzs),
            out_specs=(whole(), whole()) + (anywhere(),) * NX + (whole(),) * 2 * len(dzs),
            scratch_shapes=[
                pltpu.VMEM((2 * half, model_width), bf16),
                pltpu.VMEM((held, keep_count, block_size, block_size), bf16),
                pltpu.VMEM((shard_count, slots, tok_dev, block_size), bf16),
                pltpu.VMEM((model_width, held * block_size), bf16),
                pltpu.VMEM((wide, 2 * half), bf16),
                pltpu.VMEM((2 * half, held * block_size), bf16),
                pltpu.VMEM((NX * chunk + 1, block_size, block_size), bf16),
                pltpu.SemaphoreType.DMA((len(runs) + 2,)),
                pltpu.SemaphoreType.DMA((NX,)),
            ],
            compiler_params=pltpu.CompilerParams(vmem_limit_bytes=40 * 2**20),
            cost_estimate=SMALL,
            name="forward_and_grads" if dzs else "forward_and_block_grad",
        )(rows_flat, places, own_live, source, *runs, blocks, incoming, *dzs)
        acts.append(outs[0])
        dzs.append(outs[1])
        pieces.append(outs[2 : 2 + NX])
    grad_own, grad_sib = outs[2 + NX :]
    got = [[lax.ppermute(piece[d], "rep", shift_x(d)) for d in range(1, NX)] for piece in pieces]

    scale = 1.0 / math.sqrt(2 * half * lax.axis_size("rep"))
    along = [add_transposed([piece[0]] + parts) for piece, parts in zip(pieces, got)]
    grad_sib, along[0] = lax.optimization_barrier((grad_sib, along[0]))
    other = [lax.ppermute(part, "rep", swap_h()) for part in along]
    from_sib = lax.ppermute(grad_sib, "fsdp", swap_c())
    pair = (grad_own.astype(f32) + from_sib.astype(f32)).astype(bf16)
    pair = pair.reshape(NY, NZ * tok_dev, model_width)
    parts = [lax.ppermute(pair[d], "fsdp", shift_y(-d)) for d in range(1, NY)]
    total = pair[0].astype(f32)
    for part in parts:
        total = total + part.astype(f32)
    total = total.astype(bf16).reshape(NZ, tok_dev, model_width)

    acts, total = lax.optimization_barrier((jnp.concatenate(acts, axis=1), total))
    mines, gathered = [], []
    for part, more in zip(along, other):
        if gathered:
            more, gathered[0], total = lax.optimization_barrier((more, gathered[0], total))
        mine = ((part.astype(f32) + more.astype(f32)) * scale).astype(bf16)
        mines.append(mine)
        gathered.append(
            [mine] + [lax.ppermute(mine, "rep", shift_x(d)) for d in range(1, NX)]
        )
    returned = lax.all_to_all(acts, "fsdp", split_axis=0, concat_axis=0, tiled=True)
    parts = [lax.ppermute(total[d], "fsdp", shift_zl(-d)) for d in range(1, NZ)]
    parts, gathered[1], returned = lax.optimization_barrier((parts, gathered[1], returned))
    input_grad = total[0].astype(f32)
    for part in parts:
        input_grad = input_grad + part.astype(f32)
    input_grad = input_grad.astype(bf16)


    panel_first = jnp.sum(member * first_panel[None, :], axis=1)
    panel_slot = panel_owner * slot_count + panel_ids - panel_first
    act_panels = jnp.take(
        returned.reshape(shard_count * slot_count, tok_dev, block_size), panel_slot, axis=0
    )
    activation_out = jnp.transpose(act_panels, (1, 0, 2)).reshape(tok_dev, panel_count * block_size)

    block_grad = None
    away = jnp.arange(NX, dtype=jnp.int32)
    for (lo, hi), parts in zip(sets, gathered):
        starts = lo * keep_count + ((x_index - away) % NX) * parts[0].shape[0]
        block_grad = place(
            starts.astype(jnp.int32), slot_count * keep_count, parts, block_grad
        )
    return (activation_out, input_grad, block_grad.reshape(blocks.shape))


def solution(mesh):
    return jax.shard_map(
        per_device,
        mesh=mesh,
        in_specs=(
            P(("rep", "fsdp"), None),
            P(("rep", "fsdp"), None),
            P("fsdp", None, None, None),
            P(),
            P(),
        ),
        out_specs=(P(("rep", "fsdp"), None), P(("rep", "fsdp"), None), P("fsdp", None, None, None)),
        check_vma=False,
    )
```

```python
import functools
import math

import jax
import jax.numpy as jnp
from jax import lax
from jax.experimental import pallas as pl
from jax.experimental.pallas import tpu as pltpu
from jax.sharding import PartitionSpec as P

NZ, NY, NC = 4, 4, 2
NX, NH = 4, 2
GROUP = 16


def shift_zl(distance):
    return [
        ((z * NY + y) * NC + c, (((z + distance) % NZ) * NY + y) * NC + c)
        for z in range(NZ)
        for y in range(NY)
        for c in range(NC)
    ]


def shift_y(distance):
    return [
        ((z * NY + y) * NC + c, (z * NY + (y + distance) % NY) * NC + c)
        for z in range(NZ)
        for y in range(NY)
        for c in range(NC)
    ]


def swap_c():
    return [(k, k ^ 1) for k in range(NZ * NY * NC)]


def shift_x(distance):
    return [
        (x * NH + h, ((x + distance) % NX) * NH + h) for x in range(NX) for h in range(NH)
    ]


def swap_h():
    return [(r, r ^ 1) for r in range(NX * NH)]


def build_dense(rows_ref, first, blocks_ref, dense_ref):
    slots, keep, bs = blocks_ref.shape[0], blocks_ref.shape[1], blocks_ref.shape[2]
    for p in range(slots):
        for j in range(keep):
            at = pl.multiple_of(rows_ref[(first + p) * keep + j] * bs, bs)
            dense_ref[pl.ds(at, bs), p * bs : (p + 1) * bs] = blocks_ref[p, j]


def forward_kernel(first, slots, pieces, rows_ref, place_ref, live_ref, source_ref, *rest):
    token_hbm = rest[:pieces]
    blocks_hbm, ups_hbm = rest[pieces : pieces + 2]
    outs = rest[pieces + 2 :]
    earlier_ref = None
    if first > 0:
        earlier_ref, outs = outs[0], outs[1:]
    act_ref, dz_ref = outs[:2]
    chunk_refs, outs = outs[2 : 2 + NX], outs[2 + NX :]
    if first > 0:
        back_refs, outs = outs[:2], outs[2:]
    tok_ref, blocks_ref, ups_ref, dense_ref, dzt_ref, dzs_ref, grads_ref, in_sems, out_sems = outs
    keep, bs = blocks_ref.shape[1], blocks_ref.shape[2]
    base = blocks_ref.shape[0] - slots
    rows, width = tok_ref.shape
    row_blocks = width // bs
    part = rows // pieces
    tile, span = 512, 2048

    get_blocks = pltpu.make_async_copy(
        blocks_hbm.at[pl.ds(first - base, base + slots)], blocks_ref, in_sems.at[0]
    )
    get_ups = pltpu.make_async_copy(ups_hbm.at[:, pl.ds(first, slots)], ups_ref, in_sems.at[1])
    get_tokens = [
        pltpu.make_async_copy(
            token_hbm[i], tok_ref.at[pl.ds(i * part, part)], in_sems.at[2 + i]
        )
        for i in range(pieces)
    ]
    get_blocks.start()
    for copy in get_tokens:
        copy.start()
    get_ups.start()
    dense_ref[...] = jnp.zeros_like(dense_ref)
    get_blocks.wait()
    build_dense(rows_ref, first - base, blocks_ref, dense_ref)
    get_ups.wait()
    for copy in get_tokens:
        copy.wait()

    def step(t, carry):
        row = pl.multiple_of(t * tile, tile)
        z = jnp.dot(
            tok_ref[pl.ds(row, tile), :],
            dense_ref[:, base * bs :],
            preferred_element_type=jnp.float32,
        )
        sig = jax.nn.sigmoid(z)
        act = (z * sig).astype(jnp.bfloat16)
        slope = sig * (1.0 + z * (1.0 - sig))
        for g in range(tile // GROUP):
            src = source_ref[t * (tile // GROUP) + g]
            lo = g * GROUP
            for p in range(slots):
                cols = slice(p * bs, (p + 1) * bs)
                act_ref[src, p] = act[lo : lo + GROUP, cols]
                up = ups_ref[src, p].astype(jnp.float32) * slope[lo : lo + GROUP, cols]
                up = jnp.where(live_ref[first + p] == 1, up, 0.0)
                dz_ref[pl.ds(row + lo, GROUP), cols] = up.astype(jnp.bfloat16)
        return carry

    lax.fori_loop(0, rows // tile, step, 0)

    dzt_ref[...] = dz_ref[...].T

    def grad_step(r, carry):
        at = pl.multiple_of(r * span, span)
        grad = jnp.dot(
            dzt_ref[...], tok_ref[:, pl.ds(at, span)], preferred_element_type=jnp.float32
        ).astype(jnp.bfloat16)
        for k in range(span // bs):
            for p in range(slots):
                place = place_ref[(first + p) * row_blocks + r * (span // bs) + k]
                grads_ref[place] = grad[p * bs : (p + 1) * bs, k * bs : (k + 1) * bs]
        return carry

    lax.fori_loop(0, width // span, grad_step, 0)
    chunk = slots * keep // NX
    copies = [
        pltpu.make_async_copy(
            grads_ref.at[pl.ds(d * chunk, chunk)], chunk_refs[d], out_sems.at[d]
        )
        for d in range(NX)
    ]
    for copy in copies:
        copy.start()
    if first > 0:
        dzs_ref[:, : base * bs] = earlier_ref[...]
        dzs_ref[:, base * bs :] = dz_ref[...]
        half, wide = rows // 2, 1024

        def back_step(t, carry):
            at = pl.multiple_of(t * wide, wide)
            back = lax.dot_general(
                dzs_ref[...],
                dense_ref[pl.ds(at, wide), :],
                (((1,), (1,)), ((), ())),
                preferred_element_type=jnp.float32,
            ).astype(jnp.bfloat16)
            back_refs[0][:, pl.ds(at, wide)] = back[:half]
            back_refs[1][:, pl.ds(at, wide)] = back[half:]
            return carry

        lax.fori_loop(0, width // wide, back_step, 0)
    for copy in copies:
        copy.wait()


def add_kernel(*refs):
    out_ref = refs[-1]
    for i in range(out_ref.shape[0]):
        total = refs[0][i].astype(jnp.float32)
        for ref in refs[1:-1]:
            total = total + ref[i].astype(jnp.float32)
        out_ref[i] = total.T.astype(out_ref.dtype)


def place_kernel(count, *refs):
    start_ref = refs[0]
    part_refs, out_ref, sems = refs[1 : 1 + count], refs[-2], refs[-1]
    copies = [
        pltpu.make_async_copy(
            part, out_ref.at[pl.ds(start_ref[i], part.shape[0])], sems.at[i]
        )
        for i, part in enumerate(part_refs)
    ]
    for copy in copies:
        copy.start()
    for copy in copies:
        copy.wait()


SMALL = pl.CostEstimate(flops=1000, bytes_accessed=1000, transcendentals=0)


def anywhere():
    return pl.BlockSpec(memory_space=pl.ANY)


def add_transposed(arrays):
    return pl.pallas_call(
        add_kernel,
        out_shape=jax.ShapeDtypeStruct(arrays[0].shape, jnp.bfloat16),
        in_specs=[whole()] * len(arrays),
        out_specs=whole(),
        cost_estimate=SMALL,
        compiler_params=pltpu.CompilerParams(vmem_limit_bytes=16 * 2**20),
        name="add_along_x",
    )(*arrays)


def place(starts, total, parts, into=None):
    args = (starts, *parts) + (() if into is None else (into,))
    return pl.pallas_call(
        functools.partial(place_kernel, len(parts)),
        out_shape=jax.ShapeDtypeStruct((total,) + parts[0].shape[1:], parts[0].dtype),
        in_specs=[scalars()] + [whole()] * len(parts) + [anywhere()] * (len(args) - 1 - len(parts)),
        out_specs=anywhere(),
        input_output_aliases={} if into is None else {len(args) - 1: 0},
        scratch_shapes=[pltpu.SemaphoreType.DMA((len(parts),))],
        cost_estimate=SMALL,
        compiler_params=pltpu.CompilerParams(vmem_limit_bytes=16 * 2**20),
        name="place_blocks",
    )(*args)


def whole():
    return pl.BlockSpec(memory_space=pltpu.VMEM)


def scalars():
    return pl.BlockSpec(memory_space=pltpu.SMEM)


def per_device(tokens, upstream, blocks, keep_mask, panel_owner):
    shard_count = lax.axis_size("fsdp")
    own_index = lax.axis_index("fsdp")
    x_index = lax.axis_index("rep") // NH
    tok_dev, model_width = tokens.shape
    slot_count, keep_count, block_size = blocks.shape[0], blocks.shape[1], blocks.shape[3]
    row_blocks = keep_mask.shape[0]
    panel_count = panel_owner.shape[0]
    half = tok_dev * NZ * NY
    f32, bf16 = jnp.float32, jnp.bfloat16

    shard_ids = jnp.arange(shard_count, dtype=jnp.int32)
    member = (panel_owner[:, None] == shard_ids[None, :]).astype(jnp.int32)
    counts = jnp.sum(member, axis=0)
    first_panel = jnp.cumsum(counts) - counts
    slot_ids = jnp.arange(slot_count, dtype=jnp.int32)
    panel_table = jnp.clip(first_panel[:, None] + slot_ids[None, :], 0, panel_count - 1)
    is_mine = shard_ids == own_index
    own_first = jnp.sum(jnp.where(is_mine, first_panel, 0))
    own_count = jnp.sum(jnp.where(is_mine, counts, 0))
    own_live = (slot_ids < own_count).astype(jnp.int32)
    own_panels = jnp.clip(own_first + slot_ids, 0, panel_count - 1)
    panel_ids = jnp.arange(panel_count, dtype=jnp.int32)
    panel_pick = (panel_ids[None, :] == own_panels[:, None]).astype(jnp.int32)
    running = jnp.cumsum(keep_mask, axis=0)
    own_running = jnp.sum(panel_pick[:, None, :] * running[None, :, :], axis=2)
    own_keep = jnp.sum(panel_pick[:, None, :] * keep_mask[None, :, :], axis=2)
    pick_ids = jnp.arange(keep_count, dtype=jnp.int32)
    own_rows = jnp.sum(
        (own_running[:, :, None] <= pick_ids[None, None, :]).astype(jnp.int32), axis=1
    )
    sets = ((0, slot_count // 2), (slot_count // 2, slot_count))
    places = []
    for lo, hi in sets:
        chunk = (hi - lo) * keep_count // NX
        flat = (slot_ids[lo:hi, None] - lo) * keep_count + own_running[lo:hi] - 1
        spot = ((flat // chunk - x_index) % NX) * chunk + flat % chunk
        places.append(jnp.where(own_keep[lo:hi] == 1, spot, (hi - lo) * keep_count))
    places = jnp.concatenate(places, axis=0).reshape(-1).astype(jnp.int32)
    rows_flat = own_rows.reshape(-1).astype(jnp.int32)
    my_z, my_y, my_c = own_index // (NY * NC), (own_index // NC) % NY, own_index % NC
    away_c = jnp.arange(2, dtype=jnp.int32)[:, None, None]
    away_y = jnp.arange(NY, dtype=jnp.int32)[None, :, None]
    away_z = jnp.arange(NZ, dtype=jnp.int32)[None, None, :]
    source = (((my_z - away_z) % NZ) * NY + (my_y - away_y) % NY) * NC + (my_c + away_c) % NC
    source = source.reshape(-1).astype(jnp.int32)

    upstream_panels = jnp.transpose(upstream.reshape(tok_dev, panel_count, block_size), (1, 0, 2))
    outgoing = jnp.take(upstream_panels, panel_table.reshape(-1), axis=0)
    outgoing = outgoing.reshape(shard_count, slot_count, tok_dev, block_size)
    outgoing, tokens = lax.optimization_barrier((outgoing, tokens))
    incoming = lax.all_to_all(outgoing, "fsdp", split_axis=0, concat_axis=0, tiled=True)

    along_z = [tokens] + [lax.ppermute(tokens, "fsdp", shift_zl(d)) for d in range(1, NZ)]
    line = jnp.concatenate(along_z, axis=0)
    along_y = [line] + [lax.ppermute(line, "fsdp", shift_y(d)) for d in range(1, NY)]
    along_y[1], incoming = lax.optimization_barrier((along_y[1], incoming))
    runs = along_y + [lax.ppermute(run, "fsdp", swap_c()) for run in along_y]

    acts, dzs, pieces = [], [], []
    for lo, hi in sets:
        slots = hi - lo
        wide = slots * block_size
        chunk = slots * keep_count // NX
        held = slots + len(dzs) * lo
        outs = pl.pallas_call(
            functools.partial(forward_kernel, lo, slots, len(runs)),
            out_shape=(
                jax.ShapeDtypeStruct((shard_count, slots, tok_dev, block_size), bf16),
                jax.ShapeDtypeStruct((2 * half, wide), bf16),
            )
            + tuple(
                jax.ShapeDtypeStruct((chunk, block_size, block_size), bf16) for _ in range(NX)
            )
            + (jax.ShapeDtypeStruct((half, model_width), bf16),) * 2 * len(dzs),
            in_specs=[scalars()] * 4 + [anywhere()] * (len(runs) + 2) + [whole()] * len(dzs),
            out_specs=(whole(), whole()) + (anywhere(),) * NX + (whole(),) * 2 * len(dzs),
            scratch_shapes=[
                pltpu.VMEM((2 * half, model_width), bf16),
                pltpu.VMEM((held, keep_count, block_size, block_size), bf16),
                pltpu.VMEM((shard_count, slots, tok_dev, block_size), bf16),
                pltpu.VMEM((model_width, held * block_size), bf16),
                pltpu.VMEM((wide, 2 * half), bf16),
                pltpu.VMEM((2 * half, held * block_size), bf16),
                pltpu.VMEM((NX * chunk + 1, block_size, block_size), bf16),
                pltpu.SemaphoreType.DMA((len(runs) + 2,)),
                pltpu.SemaphoreType.DMA((NX,)),
            ],
            compiler_params=pltpu.CompilerParams(vmem_limit_bytes=40 * 2**20),
            cost_estimate=SMALL,
            name="forward_and_grads" if dzs else "forward_and_block_grad",
        )(rows_flat, places, own_live, source, *runs, blocks, incoming, *dzs)
        acts.append(outs[0])
        dzs.append(outs[1])
        pieces.append(outs[2 : 2 + NX])
    grad_own, grad_sib = outs[2 + NX :]
    got = [[lax.ppermute(piece[d], "rep", shift_x(d)) for d in range(1, NX)] for piece in pieces]

    scale = 1.0 / math.sqrt(2 * half * lax.axis_size("rep"))
    along = [add_transposed([piece[0]] + parts) for piece, parts in zip(pieces, got)]
    grad_sib, along[0] = lax.optimization_barrier((grad_sib, along[0]))
    other = [lax.ppermute(part, "rep", swap_h()) for part in along]
    from_sib = lax.ppermute(grad_sib, "fsdp", swap_c())
    pair = (grad_own.astype(f32) + from_sib.astype(f32)).astype(bf16)
    pair = pair.reshape(NY, NZ * tok_dev, model_width)
    parts = [lax.ppermute(pair[d], "fsdp", shift_y(-d)) for d in range(1, NY)]
    total = pair[0].astype(f32)
    for part in parts:
        total = total + part.astype(f32)
    total = total.astype(bf16).reshape(NZ, tok_dev, model_width)

    acts, total = lax.optimization_barrier((jnp.concatenate(acts, axis=1), total))
    mines, gathered = [], []
    for part, more in zip(along, other):
        if gathered:
            more, gathered[0], total = lax.optimization_barrier((more, gathered[0], total))
        mine = ((part.astype(f32) + more.astype(f32)) * scale).astype(bf16)
        mines.append(mine)
        gathered.append(
            [mine] + [lax.ppermute(mine, "rep", shift_x(d)) for d in range(1, NX)]
        )
    returned = lax.all_to_all(acts, "fsdp", split_axis=0, concat_axis=0, tiled=True)
    parts = [lax.ppermute(total[d], "fsdp", shift_zl(-d)) for d in range(1, NZ)]
    parts, gathered[1], returned = lax.optimization_barrier((parts, gathered[1], returned))
    input_grad = total[0].astype(f32)
    for part in parts:
        input_grad = input_grad + part.astype(f32)
    input_grad = input_grad.astype(bf16)


    panel_first = jnp.sum(member * first_panel[None, :], axis=1)
    panel_slot = panel_owner * slot_count + panel_ids - panel_first
    act_panels = jnp.take(
        returned.reshape(shard_count * slot_count, tok_dev, block_size), panel_slot, axis=0
    )
    activation_out = jnp.transpose(act_panels, (1, 0, 2)).reshape(tok_dev, panel_count * block_size)

    block_grad = None
    away = jnp.arange(NX, dtype=jnp.int32)
    for (lo, hi), parts in zip(sets, gathered):
        starts = lo * keep_count + ((x_index - away) % NX) * parts[0].shape[0]
        block_grad = place(
            starts.astype(jnp.int32), slot_count * keep_count, parts, block_grad
        )
    return (activation_out, input_grad, block_grad.reshape(blocks.shape))


def solution(mesh):
    return jax.shard_map(
        per_device,
        mesh=mesh,
        in_specs=(
            P(("rep", "fsdp"), None),
            P(("rep", "fsdp"), None),
            P("fsdp", None, None, None),
            P(),
            P(),
        ),
        out_specs=(P(("rep", "fsdp"), None), P(("rep", "fsdp"), None), P("fsdp", None, None, None)),
        check_vma=False,
    )
```
